32 devices in a mesh: fsdp: 4 (over y, core), ctx: 8 (over z, x).
Axes of the slice: x: 2, y: 2, z: 4, core: 2. Of those that a mesh axis runs over, the one named last changes fastest.
Arguments:
- token_ids: int32 [2048], P('ctx'), may hold values from 0 to 15
- table: float32 [16, 4096], P(None, 'fsdp'), may hold values from -6 to 6
- norm_gain: float32 [4096], P('fsdp'), may hold values from 0.25 to 1.75
- conv_weight: float32 [4, 4096], P(None, 'fsdp'), may hold values from -4 to 4
- conv_bias: float32 [4096], P('fsdp'), may hold values from -4 to 4
- weight_b: bfloat16 [4096, 128], P('fsdp'), may hold values from -0.09375 to 0.09375
- weight_c: bfloat16 [4096, 128], P('fsdp'), may hold values from -0.09375 to 0.09375
- step_weight: bfloat16 [4096, 64], P('fsdp'), may hold values from -0.1875 to 0.1875
- step_bias: float32 [64], P('fsdp'), as said below
- log_rate: float32 [64], P('fsdp'), as said below
- skip_gain: float32 [64], P('fsdp'), may hold values from 0.25 to 1.75
- out_grad: bfloat16 [2048, 4096], P('ctx', 'fsdp'), may hold values from -6 to 6
Outputs:
- mixer_out: bfloat16 [2048, 4096], P('ctx', 'fsdp')
- grad_embedded: bfloat16 [2048, 4096], P('ctx', 'fsdp')
- grad_table: float32 [16, 4096], P(None, 'fsdp')
- grad_norm_gain: float32 [4096], P('fsdp')
- grad_conv_weight: float32 [4, 4096], P(None, 'fsdp')
- grad_conv_bias: float32 [4096], P('fsdp')
- grad_weight_b: float32 [4096, 128], P('fsdp')
- grad_weight_c: float32 [4096, 128], P('fsdp')
- grad_step_weight: float32 [4096, 64], P('fsdp')
- grad_step_bias: float32 [64], P('fsdp')
- grad_log_rate: float32 [64], P('fsdp')
- grad_skip_gain: float32 [64], P('fsdp')
The draws below stay inside these ranges and needn't reach their ends.
Inputs may be any that keep to these rules, and one draw needn't show every extreme that they name: exp(log_rate) lies between 1 / 16 and 1 for every head. step_bias lies between log(1 / 2048) - 1 and log(0.2) - 1.
All inputs are finite; a program needn't handle non-finite values.
Results may differ from the reference program's by a relative error of at most 0.02.
Values may be sent and summed in bfloat16 or wider, within the bound.
A program may use at most 128 MiB of HBM per device.

```python
import math
import jax
import jax.numpy as jnp
from jax import lax

D = 4096
HEADS = 64
STATE = 128
VOCAB = 16
KW = 4
SPAN = 256
SEQ_LEN = 2048
N_FSDP = 4


def head_plan(key, portion):
    folded = jax.random.fold_in(key, 7)
    chooser_key, rate_key, size_key = jax.random.split(folded, 3)
    chooser = jax.random.uniform(chooser_key, (HEADS,), jnp.float32)
    rate_blend = jax.random.uniform(rate_key, (HEADS,), jnp.float32)
    size_blend = jax.random.uniform(size_key, (HEADS,), jnp.float32)
    slow_rate = math.log(0.25 / SEQ_LEN) + rate_blend * math.log(4.0)
    fast_rate = math.log(1.0 / 50.0) + rate_blend * math.log(2.0)
    slow_size = math.log(1.0 / SEQ_LEN) + size_blend * math.log(4.0)
    fast_size = math.log(0.05) + size_blend * math.log(4.0)
    slower = chooser < portion
    log_decay = jnp.where(slower, slow_rate, fast_rate)
    log_size = jnp.where(slower, slow_size, fast_size)
    return (log_decay - log_size, log_size - 1.0)


def draw_log_rate(key, part):
    portion = 0.5
    rates, biases = head_plan(key, portion)
    return rates.astype(jnp.float32)


def draw_step_bias(key, part):
    portion = 0.5
    rates, biases = head_plan(key, portion)
    return biases.astype(jnp.float32)


def draw_token_ids(key, part):
    folded = jax.random.fold_in(key, 11)
    cut_key, order_key, upper_key, rank_key, low_key, high_key = jax.random.split(folded, 6)
    quarter = SEQ_LEN // 4
    jitter_reach = SEQ_LEN // 16
    jitter = jax.random.randint(cut_key, (3,), -jitter_reach, jitter_reach + 1, dtype=jnp.int32)
    cut_points = jnp.arange(1, 4, dtype=jnp.int32) * quarter + jitter
    positions = jnp.arange(SEQ_LEN, dtype=jnp.int32)
    regime = jnp.sum((positions[:, None] >= cut_points[None, :]).astype(jnp.int32), axis=1)
    orderings = jax.vmap(lambda subkey: jax.random.permutation(subkey, VOCAB))(jax.random.split(order_key, 4))
    upper_rank = jax.random.randint(upper_key, (SEQ_LEN,), 0, VOCAB, dtype=jnp.int32)
    rank_drawn = jax.random.randint(rank_key, (SEQ_LEN,), 0, upper_rank + 1, dtype=jnp.int32)
    token_values = orderings[regime, rank_drawn].astype(jnp.int32)
    low_spot = jax.random.randint(low_key, (), 0, SEQ_LEN // 2, dtype=jnp.int32)
    high_spot = jax.random.randint(high_key, (), SEQ_LEN // 2, SEQ_LEN, dtype=jnp.int32)
    token_values = token_values.at[low_spot].set(0)
    token_values = token_values.at[high_spot].set(VOCAB - 1)
    return token_values.astype(jnp.int32)


def shard_levels(own_key, dims, cuts, low, top_value):
    def one(position, shards_of):
        steps = jax.random.uniform(jax.random.fold_in(jax.random.fold_in(own_key, 6), position), (shards_of,), jnp.float32, low / len(cuts), top_value / len(cuts))
        return jnp.repeat(jnp.exp(steps), dims[position] // shards_of).reshape((-1,) + (1,) * (len(dims) - position - 1))

    gain = one(*cuts[0])
    for cut in cuts[1:]:
        gain = gain * one(*cut)
    return gain


def gaussian(stream_key, extent, scale, bound, cuts=(), held_as=jnp.bfloat16):
    array = scale * jax.random.normal(stream_key, extent, jnp.float32)
    if cuts:
        array = array * shard_levels(stream_key, extent, cuts, -0.22, 0.18)
    return jnp.clip(array, -bound, bound).astype(held_as)


def setup_inputs(seed: int = 0) -> dict:
    key_list = jax.random.split(jax.random.key(seed), 13)
    token_ids = draw_token_ids(jax.random.fold_in(key_list[12], 71), 0)
    table = gaussian(key_list[1], (VOCAB, D), 1.0, 6.0, ((1, 4),), jnp.float32)
    norm_gain = jnp.clip(1.0 + 0.15 * jax.random.normal(key_list[2], (D,), jnp.float32), 0.25, 1.75)
    conv_weight = gaussian(key_list[3], (KW, D), 0.5, 4.0, ((1, 4),), jnp.float32)
    conv_bias = gaussian(key_list[4], (D,), 0.5, 4.0, ((0, 4),), jnp.float32)
    weight_b = gaussian(key_list[5], (D, STATE), D ** -0.5, 0.09375, ((0, 4),))
    weight_c = gaussian(key_list[6], (D, STATE), D ** -0.5, 0.09375, ((0, 4),))
    step_weight = gaussian(key_list[7], (D, HEADS), (D // 4) ** -0.5, 0.1875, ((0, 4),))
    step_bias = draw_step_bias(jax.random.fold_in(key_list[12], 71), 0)
    log_rate = draw_log_rate(jax.random.fold_in(key_list[12], 71), 0)
    skip_gain = jnp.clip(0.25 + 1.5 * jax.random.uniform(key_list[10], (HEADS,), jnp.float32) ** shard_levels(key_list[10], (HEADS,), ((0, 4),), -0.2, 0.2), 0.25, 1.75)
    out_grad = gaussian(key_list[11], (SEQ_LEN, D), 1.0, 6.0, ((0, 8), (1, 4)))
    return {"token_ids": token_ids, "table": table, "norm_gain": norm_gain, "conv_weight": conv_weight, "conv_bias": conv_bias, "weight_b": weight_b, "weight_c": weight_c, "step_weight": step_weight, "step_bias": step_bias, "log_rate": log_rate, "skip_gain": skip_gain, "out_grad": out_grad}


def round_keep(value):
    rounded = lax.optimization_barrier(value.astype(jnp.bfloat16))
    return rounded.astype(jnp.float32)

def make_normed(embedded, norm_gain):
    scale = lax.rsqrt(lax.optimization_barrier(jnp.mean(embedded * embedded, axis=-1, keepdims=True)) + 1e-05)
    return round_keep(embedded * scale * norm_gain)

def conv_pair(padded, conv_weight, conv_bias):
    radius = conv_weight.shape[0] - 1
    length = padded.shape[-2] - 2 * radius
    forward = conv_bias + jnp.zeros_like(padded[..., :length, :])
    backward = conv_bias + jnp.zeros_like(padded[..., :length, :])
    for offset in range(radius + 1):
        forward = forward + conv_weight[offset] * padded[..., radius - offset:radius - offset + length, :]
        backward = backward + conv_weight[offset] * padded[..., radius + offset:radius + offset + length, :]
    return (round_keep(jax.nn.silu(forward)), round_keep(jax.nn.silu(backward)))

def contract(form, left, right):
    return jnp.einsum(form, left.astype(jnp.float32), right.astype(jnp.float32), precision=lax.Precision.HIGHEST)

def local_terms(xvals, bvals, cvals, step_raw, step_bias, log_rate):
    total_rows = xvals.shape[0]
    heads = step_raw.shape[1]
    blocks = total_rows // SPAN
    b_half = bvals.astype(jnp.bfloat16).reshape(blocks, SPAN, -1)
    c_half = cvals.astype(jnp.bfloat16).reshape(blocks, SPAN, -1)
    steps = jax.nn.softplus(step_raw + step_bias).reshape(blocks, SPAN, heads)
    logdec = -steps * jnp.exp(log_rate)
    cumul = jnp.cumsum(logdec, axis=1)
    cumul_heads = jnp.transpose(cumul, (0, 2, 1))
    steps_heads = jnp.transpose(steps, (0, 2, 1))
    inner = contract('cqn,csn->cqs', c_half, b_half)
    lower = jnp.tril(jnp.ones((SPAN, SPAN), dtype=bool))
    spread = cumul_heads[:, :, :, None] - cumul_heads[:, :, None, :]
    decay = jnp.exp(jnp.where(lower, spread, -jnp.inf))
    mixing = (inner[:, None] * decay * steps_heads[:, :, None, :]).astype(jnp.bfloat16)
    x_half = xvals.astype(jnp.bfloat16).reshape(blocks, SPAN, heads, -1)
    intra = contract('chqs,cshp->cqhp', mixing, x_half)
    ending = cumul[:, -1:, :]
    weights = jnp.exp(ending - cumul) * steps
    b_scaled = (weights[..., None] * b_half[:, :, None, :].astype(jnp.float32)).astype(jnp.bfloat16)
    pieces = contract('cqhn,cqhp->chnp', b_scaled, x_half)
    totals = ending[:, 0, :]

    def advance(carry, inputs):
        total, piece = inputs
        return (jnp.exp(total)[:, None, None] * carry + piece, carry)
    start = jnp.zeros((heads, bvals.shape[1], xvals.shape[1] // heads), jnp.float32)
    final, entries = lax.scan(advance, start, (totals, pieces))
    device_decay = jnp.exp(lax.optimization_barrier(jnp.sum(totals, axis=0)))
    prior_decay = jnp.exp(jnp.cumsum(totals, axis=0) - totals)
    return (intra, final, device_decay, c_half, jnp.exp(cumul), entries, prior_decay)

def carried_terms(c_half, exp_cumul, entries, prior_decay, start_state):
    full_state = entries + prior_decay[:, :, None, None] * start_state[None]
    product = jnp.einsum('cqn,chnp->cqhp', c_half.astype(jnp.float32), full_state, precision=lax.Precision.HIGHEST)
    return exp_cumul[..., None] * product

def branch_output(xvals, bvals, cvals, step_raw, step_bias, log_rate):
    intra, final, device_decay, c_half, exp_cumul, entries, prior_decay = local_terms(xvals, bvals, cvals, step_raw, step_bias, log_rate)
    carried = carried_terms(c_half, exp_cumul, entries, prior_decay, jnp.zeros_like(final))
    return (intra + carried).reshape(xvals.shape)

def mixer_core(fwd_x, rev_x, fwd_b, fwd_c, fwd_step, rev_b, rev_c, rev_step, step_bias, log_rate, skip_gain):
    groups = N_FSDP
    rows = fwd_x.shape[0]
    width = fwd_x.shape[1]
    heads = skip_gain.shape[0]
    group_width = width // groups
    group_heads = heads // groups

    def split_cols(value, per):
        return jnp.transpose(value.reshape(rows, groups, per), (1, 0, 2))
    items = (split_cols(fwd_x, group_width), split_cols(rev_x, group_width), split_cols(fwd_step, group_heads), split_cols(rev_step, group_heads), step_bias.reshape(groups, group_heads), log_rate.reshape(groups, group_heads))

    def one_group(member):
        fx, rx, fs, rs, bias_part, rate_part = member
        forward_y = branch_output(fx, fwd_b, fwd_c, fs, bias_part, rate_part)
        reverse_y = jnp.flip(branch_output(jnp.flip(rx, 0), jnp.flip(rev_b, 0), jnp.flip(rev_c, 0), jnp.flip(rs, 0), bias_part, rate_part), 0)
        return forward_y + reverse_y
    outputs = lax.map(one_group, items)
    mixed = jnp.transpose(outputs, (1, 0, 2)).reshape(rows, width)
    per_channel = jnp.repeat(skip_gain, width // heads)
    return mixed + per_channel * (fwd_x + rev_x)

def reference(token_ids, table, norm_gain, conv_weight, conv_bias, weight_b, weight_c, step_weight, step_bias, log_rate, skip_gain, out_grad):
    onehot = (token_ids[:, None] == jnp.arange(table.shape[0])[None, :]).astype(jnp.float32)
    embedded = jnp.dot(onehot, table, precision=lax.Precision.HIGHEST)

    def front(embedded, norm_gain, conv_weight, conv_bias):
        normed = make_normed(embedded, norm_gain)
        radius = conv_weight.shape[0] - 1
        padded = jnp.pad(normed, ((radius, radius), (0, 0)))
        return conv_pair(padded, conv_weight, conv_bias)
    (fwd_x, rev_x), front_back = jax.vjp(front, embedded, norm_gain, conv_weight, conv_bias)
    fwd_half = fwd_x.astype(jnp.bfloat16)
    rev_half = rev_x.astype(jnp.bfloat16)

    def project(half):
        return (jnp.dot(half, weight_b, preferred_element_type=jnp.float32), jnp.dot(half, weight_c, preferred_element_type=jnp.float32), jnp.dot(half, step_weight, preferred_element_type=jnp.float32))
    fwd_b, fwd_c, fwd_step = project(fwd_half)
    rev_b, rev_c, rev_step = project(rev_half)
    mixed, core_back = jax.vjp(mixer_core, fwd_x, rev_x, fwd_b, fwd_c, fwd_step, rev_b, rev_c, rev_step, step_bias, log_rate, skip_gain)
    grads = core_back(out_grad.astype(jnp.float32))
    d_fx, d_rx, d_fb, d_fc, d_fs, d_rb, d_rc, d_rs, d_bias, d_rate, d_skip = grads

    def project_back(half, d_b, d_c, d_s):
        b_half = d_b.astype(jnp.bfloat16)
        c_half = d_c.astype(jnp.bfloat16)
        s_half = d_s.astype(jnp.bfloat16)
        into_x = jnp.dot(b_half, weight_b.T, preferred_element_type=jnp.float32) + jnp.dot(c_half, weight_c.T, preferred_element_type=jnp.float32) + jnp.dot(s_half, step_weight.T, preferred_element_type=jnp.float32)
        return (into_x, jnp.dot(half.T, b_half, preferred_element_type=jnp.float32), jnp.dot(half.T, c_half, preferred_element_type=jnp.float32), jnp.dot(half.T, s_half, preferred_element_type=jnp.float32))
    into_f, gb_f, gc_f, gs_f = project_back(fwd_half, d_fb, d_fc, d_fs)
    into_r, gb_r, gc_r, gs_r = project_back(rev_half, d_rb, d_rc, d_rs)
    d_embedded, d_gain, d_cw, d_cb = front_back((d_fx + into_f, d_rx + into_r))
    grad_table = jnp.dot(onehot.T, d_embedded, precision=lax.Precision.HIGHEST)
    return (mixed.astype(jnp.bfloat16), d_embedded.astype(jnp.bfloat16), grad_table, d_gain, d_cw, d_cb, gb_f + gb_r, gc_f + gc_r, gs_f + gs_r, d_bias, d_rate, d_skip)
```

```python
import functools

import jax
import jax.numpy as jnp
from jax import lax
from jax.experimental import pallas as pl
from jax.experimental.pallas import tpu as pltpu
from jax.sharding import PartitionSpec as P

F32 = jnp.float32
BF = jnp.bfloat16
HI = lax.Precision.HIGHEST
VMEM_LIMIT = 56 * 1024 * 1024


def dot(a, b, ca=1, cb=0, precision=None):
    return lax.dot_general(
        a, b, (((ca,), (cb,)), ((), ())), precision=precision, preferred_element_type=F32
    )


def split_dot(value, sel, cb=0):
    hi = value.astype(BF)
    lo = (value - hi.astype(F32)).astype(BF)
    return dot(hi, sel, 1, cb) + dot(lo, sel, 1, cb)


def softplus(v):
    return jnp.maximum(v, 0.0) + jnp.log1p(jnp.exp(-jnp.abs(v)))


def selector(heads, width):
    per = width // heads
    row = lax.broadcasted_iota(jnp.int32, (heads, width), 0)
    col = lax.broadcasted_iota(jnp.int32, (heads, width), 1)
    return jnp.where((col >= row * per) & (col < row * per + per), 1.0, 0.0).astype(BF)


def order_mask(rows, reverse):
    t = lax.broadcasted_iota(jnp.int32, (rows, rows), 0)
    s = lax.broadcasted_iota(jnp.int32, (rows, rows), 1)
    return (s >= t) if reverse else (s <= t)


def whole_kernel(fn, outs, args):
    count = len(args)

    def body(*refs):
        results = fn(*[r[...] for r in refs[:count]])
        for ref, value in zip(refs[count:], results):
            ref[...] = value.astype(ref.dtype)

    return pl.pallas_call(
        body,
        out_shape=tuple(jax.ShapeDtypeStruct(s, d) for s, d in outs),
        compiler_params=pltpu.CompilerParams(vmem_limit_bytes=VMEM_LIMIT),
    )(*args)


def states_stage(raw_f, raw_r, bias, log_rate, xf, xr, bf, cf, br, cr, dy):
    rows, heads = raw_f.shape
    sel = selector(heads, xf.shape[1])
    rate = jnp.exp(log_rate)
    cols = []
    states = []
    dstates = []
    for raw, x, b, c, reverse in ((raw_f, xf, bf, cf, False), (raw_r, xr, br, cr, True)):
        step = softplus(raw + bias)
        logdec = -step * rate
        tri = jnp.where(order_mask(rows, reverse), 1.0, 0.0)
        cumul = dot(tri, logdec, precision=HI)
        end = jnp.sum(logdec, axis=0, keepdims=True)
        wt = jnp.exp(end - cumul) * step
        xs = (split_dot(wt, sel) * x.astype(F32)).astype(BF)
        states.append(dot(b, xs, 0, 0))
        gy = (split_dot(jnp.exp(cumul), sel) * dy.astype(F32)).astype(BF)
        dstates.append(dot(c, gy, 0, 0))
        cols += [cumul, step, end]
    return (
        jnp.stack(states + dstates),
        cols[0],
        cols[1],
        cols[2],
        cols[3],
        cols[4],
        cols[5],
    )


def intra_kernel(cols_ref, cut_ref, xf_ref, xr_ref, dy_ref, bf_ref, cf_ref, br_ref, cr_ref,
                 yf_ref, yr_ref, pf_ref, pr_ref, df_ref, dr_ref, inner_f, inner_r):
    rows = xf_ref.shape[0]
    per = xf_ref.shape[1] // 2

    @pl.when(pl.program_id(0) == 0)
    def _():
        inner_f[...] = dot(cf_ref[...], bf_ref[...], 1, 1)
        inner_r[...] = dot(cr_ref[...], br_ref[...], 1, 1)
        df_ref[...] = jnp.zeros_like(df_ref)
        dr_ref[...] = jnp.zeros_like(dr_ref)

    dy = dy_ref[...]
    lane = lax.broadcasted_iota(jnp.int32, dy.shape, 1)
    zero = jnp.zeros_like(dy)
    cols = cols_ref[0]
    cut = cut_ref[0]
    for branch, (x_ref, inner, y_ref, p_ref, d_ref) in enumerate(
        ((xf_ref, inner_f, yf_ref, pf_ref, df_ref), (xr_ref, inner_r, yr_ref, pr_ref, dr_ref))
    ):
        mask = order_mask(rows, branch == 1)
        st = jnp.where(
            lane < per,
            cols[:, 4 + 2 * branch : 5 + 2 * branch],
            cols[:, 5 + 2 * branch : 6 + 2 * branch],
        )
        xs = (st * x_ref[...].astype(F32)).astype(BF)
        y = None
        p = None
        total = d_ref[...]
        for k in range(2):
            mine = (lane < per) if k == 0 else (lane >= per)
            at = 2 * branch + k
            spread = cols[:, at : at + 1] - cut[at : at + 1, :]
            decay = jnp.exp(jnp.where(mask, spread, -1e30))
            mixing = (inner[...] * decay).astype(BF)
            xs_k = jnp.where(mine, xs, zero)
            dy_k = jnp.where(mine, dy, zero)
            y_k = dot(mixing, xs_k)
            p_k = dot(mixing, dy_k, 0, 0)
            total = total + dot(dy, xs_k, 1, 1) * decay
            y = y_k if y is None else y + y_k
            p = p_k if p is None else p + p_k
        y_ref[...] = y
        p_ref[...] = p
        d_ref[...] = total


def intra_stage(cols, cut, xf, xr, dy, bf, cf, br, cr):
    rows, width = xf.shape
    pairs = cols.shape[0]
    lanes = width // pairs
    wide = pl.BlockSpec((rows, lanes), lambda j: (0, j))
    small = pl.BlockSpec(bf.shape, lambda j: (0, 0))
    square = pl.BlockSpec((rows, rows), lambda j: (0, 0))
    return pl.pallas_call(
        intra_kernel,
        grid=(pairs,),
        in_specs=[
            pl.BlockSpec((1, rows, 8), lambda j: (j, 0, 0)),
            pl.BlockSpec((1, 4, rows), lambda j: (j, 0, 0)),
            wide,
            wide,
            wide,
            small,
            small,
            small,
            small,
        ],
        out_specs=[wide, wide, wide, wide, square, square],
        out_shape=[jax.ShapeDtypeStruct((rows, width), F32)] * 4
        + [jax.ShapeDtypeStruct((rows, rows), F32)] * 2,
        scratch_shapes=[pltpu.VMEM((rows, rows), F32), pltpu.VMEM((rows, rows), F32)],
        compiler_params=pltpu.CompilerParams(vmem_limit_bytes=VMEM_LIMIT),
    )(cols, cut, xf, xr, dy, bf, cf, br, cr)


def joined_stage(chained, yf, yr, pf, pr, df, dr, xf, xr, dy_half, bf, cf, br, cr,
                 raw_f, raw_r, cum_f, cum_r, bias, log_rate, skip):
    rows, heads = raw_f.shape
    sel = selector(heads, xf.shape[1])
    rate = jnp.exp(log_rate)
    dy = dy_half.astype(F32)
    channel = split_dot(jnp.broadcast_to(skip, (8, heads)), sel)[:1]
    both = xf.astype(F32) + xr.astype(F32)
    mixed = channel * both
    direct = channel * dy
    d_skip = jnp.sum(split_dot(dy * both, sel, 1), axis=0, keepdims=True)
    results = []
    d_bias = 0.0
    d_rate = 0.0
    for k, (intra, p, square, x_half, b, c, raw, cumul) in enumerate(
        ((yf, pf, df, xf, bf, cf, raw_f, cum_f), (yr, pr, dr, xr, br, cr, raw_r, cum_r))
    ):
        reverse = k == 1
        start = chained[k]
        leaving = chained[2 + k]
        x = x_half.astype(F32)
        shifted = raw + bias
        step = softplus(shifted)
        logdec = -step * rate
        end = jnp.sum(logdec, axis=0, keepdims=True)
        grow = split_dot(jnp.exp(cumul), sel)
        fade = split_dot(jnp.exp(end - cumul), sel)
        wide_step = split_dot(step, sel)
        start_half = start.astype(BF)
        leaving_half = leaving.astype(BF)
        y = intra + grow * dot(c, start_half)
        mixed = mixed + y
        state_back = fade * dot(b, leaving_half)
        q = p + state_back
        x_step = wide_step * x
        d_x = wide_step * q + direct
        square_half = square.astype(BF)
        gy = (grow * dy).astype(BF)
        d_c = dot(square_half, b) + dot(gy, start_half, 1, 1)
        xs2 = (x_step * fade).astype(BF)
        d_b = dot(square_half, c, 0, 0) + dot(xs2, leaving_half, 1, 1)
        d_step = split_dot(x * q, sel, 1)
        through = split_dot(x_step * state_back, sel, 1)
        own = x_step.astype(BF).astype(F32) * p
        d_cumul = split_dot(dy * y - own, sel, 1) - through
        pair = split_dot(leaving * start, sel, 1)
        d_end = jnp.sum(through, axis=0, keepdims=True) + jnp.exp(end) * jnp.sum(
            pair, axis=0, keepdims=True
        )
        tri = jnp.where(order_mask(rows, reverse), 1.0, 0.0)
        d_log = dot(tri, d_cumul, 0, 0, precision=HI) + d_end
        d_step = d_step - rate * d_log
        d_raw = d_step / (1.0 + jnp.exp(-shifted))
        d_bias = d_bias + jnp.sum(d_raw, axis=0, keepdims=True)
        d_rate = d_rate + jnp.sum(d_log * logdec, axis=0, keepdims=True)
        results.append((d_x, d_b, d_c, d_raw))
    (fx, fb, fc, fs), (rx, rb, rc, rs) = results
    return mixed, fx, rx, jnp.stack([fb, fc, rb, rc]), jnp.stack([fs, rs]), d_bias, d_rate, d_skip


def chain_weights(totals, here, forward):
    count = totals.shape[0]
    k = jnp.arange(count)[:, None]
    j = jnp.arange(count)[None, :]
    if forward:
        between = (j > k) & (j < here)
        reached = jnp.arange(count) < here
    else:
        between = (j < k) & (j > here)
        reached = jnp.arange(count) > here
    logs = jnp.sum(jnp.where(between[:, :, None], totals[None], 0.0), axis=1)
    return jnp.where(reached[:, None], jnp.exp(logs), 0.0)


def neighbours(value, axis, steps):
    count = lax.axis_size(axis)
    first, last = (max(0, -steps), min(count, count - steps))
    return lax.ppermute(value, axis, [(source, source + steps) for source in range(first, last)])


def round_keep(value):
    rounded = lax.optimization_barrier(value.astype(BF))
    return rounded.astype(F32)


def conv_pair(padded, conv_weight, conv_bias):
    radius = conv_weight.shape[0] - 1
    length = padded.shape[0] - 2 * radius
    forward = conv_bias
    backward = conv_bias
    for k in range(radius + 1):
        forward = forward + conv_weight[k] * padded[radius - k : radius - k + length]
        backward = backward + conv_weight[k] * padded[radius + k : radius + k + length]
    return forward, backward


def local(token_ids, table, norm_gain, conv_weight, conv_bias, weight_b, weight_c, step_weight,
          step_bias, log_rate, skip_gain, out_grad):
    rows = token_ids.shape[0]
    width = table.shape[1]
    vocab = table.shape[0]
    heads = step_bias.shape[0]
    state = weight_b.shape[1]
    features = width * lax.axis_size("fsdp")
    all_heads = step_weight.shape[1]
    radius = conv_weight.shape[0] - 1
    here = lax.axis_index("ctx")

    table_sums = lax.psum(jnp.sum(table * table, axis=1), "fsdp")
    marked = token_ids + 1
    before = neighbours(marked[rows - radius :], "ctx", 1)
    after = neighbours(marked[:radius], "ctx", -1)
    marks = jnp.concatenate([before, marked, after])
    inverse = lax.rsqrt(table_sums / features + 1e-05)[:, None]
    unit_table = table * inverse
    normed_table = (unit_table * norm_gain).astype(BF)
    onehot_pad = (marks[:, None] == jnp.arange(1, vocab + 1)[None, :]).astype(BF)
    padded = dot(onehot_pad, normed_table)
    pre_f, pre_r = conv_pair(padded, conv_weight, conv_bias)
    xf = jax.nn.silu(pre_f).astype(BF)
    xr = jax.nn.silu(pre_r).astype(BF)
    joined_w = jnp.concatenate([weight_b, weight_c, step_weight], axis=1)
    both_x = jnp.concatenate([xf, xr], axis=0)
    parts = lax.psum(dot(both_x, joined_w), "fsdp")
    first_head = lax.axis_index("fsdp") * heads
    half = parts[:, : 2 * state].astype(BF)
    raws = lax.dynamic_slice_in_dim(parts[:, 2 * state :], first_head, heads, 1)
    bf, cf = half[:rows, :state], half[:rows, state:]
    br, cr = half[rows:, :state], half[rows:, state:]
    raw_f, raw_r = raws[:rows], raws[rows:]
    bias = step_bias[None]
    rate = log_rate[None]
    small = ((rows, heads), F32)
    one = ((1, heads), F32)
    states, cum_f, step_f, end_f, cum_r, step_r, end_r = whole_kernel(
        states_stage,
        [((4, state, width), BF), small, small, one, small, small, one],
        (raw_f, raw_r, bias, rate, xf, xr, bf, cf, br, cr, out_grad),
    )
    ends = lax.all_gather(jnp.concatenate([end_f, end_r]), "ctx")
    everything = lax.all_gather(states, "ctx")
    pairs = heads // 2

    def paired(value):
        return jnp.transpose(value.reshape(rows, pairs, 2), (1, 0, 2))

    cols = jnp.concatenate([paired(v) for v in (cum_f, cum_r, step_f, step_r)], axis=2)
    cut = jnp.transpose(cols[:, :, :4], (0, 2, 1))
    yf, yr, pf, pr, df, dr = intra_stage(cols, cut, xf, xr, out_grad, bf, cf, br, cr)
    weights = jnp.stack(
        [
            chain_weights(ends[:, 0], here, True),
            chain_weights(ends[:, 1], here, False),
            chain_weights(ends[:, 0], here, False),
            chain_weights(ends[:, 1], here, True),
        ],
        axis=1,
    )
    weights = jnp.repeat(weights, width // heads, axis=2)[:, :, None, :]
    chained = jnp.sum(everything.astype(F32) * weights, axis=0)
    mixer_out, d_fx, d_rx, d_bc, d_raw, d_bias, d_rate, d_skip = whole_kernel(
        joined_stage,
        [
            ((rows, width), BF),
            ((rows, width), F32),
            ((rows, width), F32),
            ((4, rows, state), BF),
            ((2, rows, heads), BF),
            one,
            one,
            one,
        ],
        (chained, yf, yr, pf, pr, df, dr, xf, xr, out_grad, bf, cf, br, cr, raw_f, raw_r,
         cum_f, cum_r, bias, rate, skip_gain[None]),
    )
    summed_bc = lax.psum(d_bc, "fsdp")
    every_raw = lax.all_gather(d_raw, "fsdp", axis=2, tiled=True)
    back = jnp.concatenate(
        [
            jnp.concatenate([summed_bc[0], summed_bc[1], every_raw[0]], axis=1),
            jnp.concatenate([summed_bc[2], summed_bc[3], every_raw[1]], axis=1),
        ],
        axis=0,
    )
    into = dot(back, joined_w, 1, 1)
    grad_w = lax.psum(dot(both_x, back, 0, 0), "ctx")

    def silu_back(pre, d_x):
        gate = jax.nn.sigmoid(pre)
        return d_x.astype(BF).astype(F32) * (gate * (1.0 + pre * (1.0 - gate)))

    pre_f, pre_r = conv_pair(padded, conv_weight, conv_bias)
    dp_f = silu_back(pre_f, d_fx + into[:rows])
    dp_r = silu_back(pre_r, d_rx + into[rows:])
    d_cb = jnp.sum(dp_f + dp_r, axis=0)
    d_cw = jnp.stack(
        [
            jnp.sum(
                dp_f * padded[radius - k : radius - k + rows]
                + dp_r * padded[radius + k : radius + k + rows],
                axis=0,
            )
            for k in range(radius + 1)
        ]
    )
    dp_f_after = neighbours(dp_f[:radius], "ctx", -1)
    dp_r_before = neighbours(dp_r[rows - radius :], "ctx", 1)
    long_f = jnp.concatenate([dp_f, dp_f_after], axis=0)
    long_r = jnp.concatenate([dp_r_before, dp_r], axis=0)
    center = 0.0
    for k in range(radius + 1):
        center = center + conv_weight[k] * (
            long_f[k : k + rows] + long_r[radius - k : radius - k + rows]
        )
    grad_normed = round_keep(center)
    onehot = (token_ids[:, None] == jnp.arange(vocab)[None, :]).astype(F32)
    scale = jnp.sum(onehot * inverse[:, 0], axis=1, keepdims=True)
    embedded = jnp.dot(onehot, table, precision=HI)
    grad_unit = grad_normed * norm_gain
    cross = lax.psum(jnp.sum(grad_unit * embedded, axis=1), "fsdp")[:, None]
    d_embedded = scale * grad_unit - embedded * (scale * scale * scale) * (cross / features)
    grad_embedded = d_embedded.astype(BF)
    d_table = jnp.dot(onehot.T, d_embedded, precision=HI)
    d_gain = jnp.sum(grad_normed * (embedded * scale), axis=0)
    wide = jnp.concatenate([d_table, d_gain[None], d_cw, d_cb[None]], axis=0)
    tiny = jnp.concatenate([d_bias, d_rate, d_skip], axis=0)
    wide, tiny = lax.psum((wide, tiny), "ctx")
    return (
        mixer_out,
        grad_embedded,
        wide[:vocab],
        wide[vocab],
        wide[vocab + 1 : vocab + 2 + radius],
        wide[vocab + 2 + radius],
        grad_w[:, :state],
        grad_w[:, state : 2 * state],
        grad_w[:, 2 * state :],
        tiny[0],
        tiny[1],
        tiny[2],
    )


def solution(mesh):
    return jax.shard_map(
        local,
        mesh=mesh,
        in_specs=(
            P("ctx"),
            P(None, "fsdp"),
            P("fsdp"),
            P(None, "fsdp"),
            P("fsdp"),
            P("fsdp", None),
            P("fsdp", None),
            P("fsdp", None),
            P("fsdp"),
            P("fsdp"),
            P("fsdp"),
            P("ctx", "fsdp"),
        ),
        out_specs=(
            P("ctx", "fsdp"),
            P("ctx", "fsdp"),
            P(None, "fsdp"),
            P("fsdp"),
            P(None, "fsdp"),
            P("fsdp"),
            P("fsdp", None),
            P("fsdp", None),
            P("fsdp", None),
            P("fsdp"),
            P("fsdp"),
            P("fsdp"),
        ),
        check_vma=False,
    )
```

```python
import functools

import jax
import jax.numpy as jnp
from jax import lax
from jax.experimental import pallas as pl
from jax.experimental.pallas import tpu as pltpu
from jax.sharding import PartitionSpec as P

F32 = jnp.float32
BF = jnp.bfloat16
HI = lax.Precision.HIGHEST
VMEM_LIMIT = 56 * 1024 * 1024


def dot(a, b, ca=1, cb=0, precision=None):
    return lax.dot_general(
        a, b, (((ca,), (cb,)), ((), ())), precision=precision, preferred_element_type=F32
    )


def split_dot(value, sel, cb=0):
    hi = value.astype(BF)
    lo = (value - hi.astype(F32)).astype(BF)
    return dot(hi, sel, 1, cb) + dot(lo, sel, 1, cb)


def softplus(v):
    return jnp.maximum(v, 0.0) + jnp.log1p(jnp.exp(-jnp.abs(v)))


def selector(heads, width):
    per = width // heads
    row = lax.broadcasted_iota(jnp.int32, (heads, width), 0)
    col = lax.broadcasted_iota(jnp.int32, (heads, width), 1)
    return jnp.where((col >= row * per) & (col < row * per + per), 1.0, 0.0).astype(BF)


def order_mask(rows, reverse):
    t = lax.broadcasted_iota(jnp.int32, (rows, rows), 0)
    s = lax.broadcasted_iota(jnp.int32, (rows, rows), 1)
    return (s >= t) if reverse else (s <= t)


def whole_kernel(fn, outs, args):
    count = len(args)

    def body(*refs):
        results = fn(*[r[...] for r in refs[:count]])
        for ref, value in zip(refs[count:], results):
            ref[...] = value.astype(ref.dtype)

    return pl.pallas_call(
        body,
        out_shape=tuple(jax.ShapeDtypeStruct(s, d) for s, d in outs),
        compiler_params=pltpu.CompilerParams(vmem_limit_bytes=VMEM_LIMIT),
    )(*args)


def states_stage(raw_f, raw_r, bias, log_rate, xf, xr, bf, cf, br, cr, dy):
    rows, heads = raw_f.shape
    sel = selector(heads, xf.shape[1])
    rate = jnp.exp(log_rate)
    cols = []
    states = []
    dstates = []
    for raw, x, b, c, reverse in ((raw_f, xf, bf, cf, False), (raw_r, xr, br, cr, True)):
        step = softplus(raw + bias)
        logdec = -step * rate
        tri = jnp.where(order_mask(rows, reverse), 1.0, 0.0)
        cumul = dot(tri, logdec, precision=HI)
        end = jnp.sum(logdec, axis=0, keepdims=True)
        wt = jnp.exp(end - cumul) * step
        xs = (split_dot(wt, sel) * x.astype(F32)).astype(BF)
        states.append(dot(b, xs, 0, 0))
        gy = (split_dot(jnp.exp(cumul), sel) * dy.astype(F32)).astype(BF)
        dstates.append(dot(c, gy, 0, 0))
        wide_end = split_dot(jnp.broadcast_to(jnp.exp(end), (8, heads)), sel)
        cols += [cumul, step, wide_end]
    return (jnp.stack(states + dstates),) + tuple(cols)


def intra_kernel(cols_ref, cut_ref, xf_ref, xr_ref, dy_ref, bf_ref, cf_ref, br_ref, cr_ref,
                 yf_ref, yr_ref, pf_ref, pr_ref, df_ref, dr_ref, inner_f, inner_r):
    rows = xf_ref.shape[0]
    per = xf_ref.shape[1] // 2

    @pl.when(pl.program_id(0) == 0)
    def _():
        inner_f[...] = dot(cf_ref[...], bf_ref[...], 1, 1)
        inner_r[...] = dot(cr_ref[...], br_ref[...], 1, 1)
        df_ref[...] = jnp.zeros_like(df_ref)
        dr_ref[...] = jnp.zeros_like(dr_ref)

    dy = dy_ref[...]
    lane = lax.broadcasted_iota(jnp.int32, dy.shape, 1)
    zero = jnp.zeros_like(dy)
    cols = cols_ref[0]
    cut = cut_ref[0]
    for branch, (x_ref, inner, y_ref, p_ref, d_ref) in enumerate(
        ((xf_ref, inner_f, yf_ref, pf_ref, df_ref), (xr_ref, inner_r, yr_ref, pr_ref, dr_ref))
    ):
        mask = order_mask(rows, branch == 1)
        st = jnp.where(
            lane < per,
            cols[:, 4 + 2 * branch : 5 + 2 * branch],
            cols[:, 5 + 2 * branch : 6 + 2 * branch],
        )
        xs = (st * x_ref[...].astype(F32)).astype(BF)
        y = None
        p = None
        total = d_ref[...]
        for k in range(2):
            mine = (lane < per) if k == 0 else (lane >= per)
            at = 2 * branch + k
            spread = cols[:, at : at + 1] - cut[at : at + 1, :]
            decay = jnp.exp(jnp.where(mask, spread, -1e30))
            mixing = (inner[...] * decay).astype(BF)
            xs_k = jnp.where(mine, xs, zero)
            dy_k = jnp.where(mine, dy, zero)
            y_k = dot(mixing, xs_k)
            p_k = dot(mixing, dy_k, 0, 0)
            total = total + dot(dy, xs_k, 1, 1) * decay
            y = y_k if y is None else y + y_k
            p = p_k if p is None else p + p_k
        y_ref[...] = y
        p_ref[...] = p
        d_ref[...] = total


def intra_stage(cols, cut, xf, xr, dy, bf, cf, br, cr):
    rows, width = xf.shape
    pairs = cols.shape[0]
    lanes = width // pairs
    wide = pl.BlockSpec((rows, lanes), lambda j: (0, j))
    small = pl.BlockSpec(bf.shape, lambda j: (0, 0))
    square = pl.BlockSpec((rows, rows), lambda j: (0, 0))
    return pl.pallas_call(
        intra_kernel,
        grid=(pairs,),
        in_specs=[
            pl.BlockSpec((1, rows, 8), lambda j: (j, 0, 0)),
            pl.BlockSpec((1, 4, rows), lambda j: (j, 0, 0)),
            wide,
            wide,
            wide,
            small,
            small,
            small,
            small,
        ],
        out_specs=[wide, wide, wide, wide, square, square],
        out_shape=[jax.ShapeDtypeStruct((rows, width), F32)] * 4
        + [jax.ShapeDtypeStruct((rows, rows), F32)] * 2,
        scratch_shapes=[pltpu.VMEM((rows, rows), F32), pltpu.VMEM((rows, rows), F32)],
        compiler_params=pltpu.CompilerParams(vmem_limit_bytes=VMEM_LIMIT),
    )(cols, cut, xf, xr, dy, bf, cf, br, cr)


def joined_stage(chained, yf, yr, pf, pr, df, dr, xf, xr, dy_half, bf, cf, br, cr,
                 raw_f, raw_r, cum_f, cum_r, bias, log_rate, skip):
    rows, heads = raw_f.shape
    sel = selector(heads, xf.shape[1])
    rate = jnp.exp(log_rate)
    dy = dy_half.astype(F32)
    channel = split_dot(jnp.broadcast_to(skip, (8, heads)), sel)[:1]
    both = xf.astype(F32) + xr.astype(F32)
    mixed = channel * both
    direct = channel * dy
    d_skip = jnp.sum(split_dot(dy * both, sel, 1), axis=0, keepdims=True)
    results = []
    d_bias = 0.0
    d_rate = 0.0
    for k, (intra, p, square, x_half, b, c, raw, cumul) in enumerate(
        ((yf, pf, df, xf, bf, cf, raw_f, cum_f), (yr, pr, dr, xr, br, cr, raw_r, cum_r))
    ):
        reverse = k == 1
        start = chained[k]
        leaving = chained[2 + k]
        x = x_half.astype(F32)
        shifted = raw + bias
        step = softplus(shifted)
        logdec = -step * rate
        end = jnp.sum(logdec, axis=0, keepdims=True)
        grow = split_dot(jnp.exp(cumul), sel)
        fade = split_dot(jnp.exp(end - cumul), sel)
        wide_step = split_dot(step, sel)
        start_half = start.astype(BF)
        leaving_half = leaving.astype(BF)
        y = intra + grow * dot(c, start_half)
        mixed = mixed + y
        state_back = fade * dot(b, leaving_half)
        q = p + state_back
        x_step = wide_step * x
        d_x = wide_step * q + direct
        square_half = square.astype(BF)
        gy = (grow * dy).astype(BF)
        d_c = dot(square_half, b) + dot(gy, start_half, 1, 1)
        xs2 = (x_step * fade).astype(BF)
        d_b = dot(square_half, c, 0, 0) + dot(xs2, leaving_half, 1, 1)
        d_step = split_dot(x * q, sel, 1)
        through = split_dot(x_step * state_back, sel, 1)
        own = x_step.astype(BF).astype(F32) * p
        d_cumul = split_dot(dy * y - own, sel, 1) - through
        pair = split_dot(leaving * start, sel, 1)
        d_end = jnp.sum(through, axis=0, keepdims=True) + jnp.exp(end) * jnp.sum(
            pair, axis=0, keepdims=True
        )
        tri = jnp.where(order_mask(rows, reverse), 1.0, 0.0)
        d_log = dot(tri, d_cumul, 0, 0, precision=HI) + d_end
        d_step = d_step - rate * d_log
        d_raw = d_step / (1.0 + jnp.exp(-shifted))
        d_bias = d_bias + jnp.sum(d_raw, axis=0, keepdims=True)
        d_rate = d_rate + jnp.sum(d_log * logdec, axis=0, keepdims=True)
        results.append((d_x, d_b, d_c, d_raw))
    (fx, fb, fc, fs), (rx, rb, rc, rs) = results
    return mixed, fx, rx, jnp.stack([fb, fc, rb, rc]), jnp.stack([fs, rs]), d_bias, d_rate, d_skip


MESH = pl.DeviceIdType.MESH


def greet_all(axis, count, here):
    barrier = pltpu.get_barrier_semaphore()
    for d in range(1, count):
        pl.semaphore_signal(
            barrier, inc=1, device_id={axis: lax.rem(here + d, count)}, device_id_type=MESH
        )
    pl.semaphore_wait(barrier, count - 1)


def exchange(arrays, modes, axis, collective_id):
    count = lax.axis_size(axis)
    many = len(arrays)

    def body(*refs):
        ins, outs, bufs = refs[:many], refs[many : 2 * many], refs[2 * many : 3 * many]
        send, recv = refs[3 * many :]
        here = lax.axis_index(axis)
        greet_all(axis, count, here)
        copies = []
        for d in range(1, count):
            for k in range(many):
                copy = pltpu.make_async_remote_copy(
                    src_ref=ins[k],
                    dst_ref=bufs[k].at[d - 1],
                    send_sem=send.at[k, d - 1],
                    recv_sem=recv.at[k, d - 1],
                    device_id={axis: lax.rem(here + d, count)},
                    device_id_type=MESH,
                )
                copy.start()
                copies.append(copy)
        for copy in copies:
            copy.wait()
        for k in range(many):
            if modes[k] == "sum":
                total = ins[k][...].astype(F32)
                for d in range(1, count):
                    total = total + bufs[k][d - 1].astype(F32)
                outs[k][...] = total.astype(outs[k].dtype)
            else:
                outs[k][here] = ins[k][...]
                for d in range(1, count):
                    outs[k][lax.rem(here - d + count, count)] = bufs[k][d - 1]

    shapes = [
        jax.ShapeDtypeStruct(a.shape if m == "sum" else (count,) + a.shape, a.dtype)
        for a, m in zip(arrays, modes)
    ]
    return pl.pallas_call(
        body,
        out_shape=tuple(shapes),
        in_specs=[pl.BlockSpec(memory_space=pltpu.VMEM)] * many,
        out_specs=tuple([pl.BlockSpec(memory_space=pltpu.VMEM)] * many),
        scratch_shapes=[pltpu.VMEM((count - 1,) + a.shape, a.dtype) for a in arrays]
        + [pltpu.SemaphoreType.DMA((many, count - 1)), pltpu.SemaphoreType.DMA((many, count - 1))],
        compiler_params=pltpu.CompilerParams(
            collective_id=collective_id, has_side_effects=True, vmem_limit_bytes=VMEM_LIMIT
        ),
    )(*arrays)


def reduce_all(arrays, axis, collective_id):
    count = lax.axis_size(axis)
    many = len(arrays)
    chunks = [a.shape[0] // count for a in arrays]

    def body(*refs):
        ins, outs = refs[:many], refs[many : 2 * many]
        first, second = refs[2 * many : 3 * many], refs[3 * many : 4 * many]
        mine = refs[4 * many : 5 * many]
        send1, recv1, send2, recv2 = refs[5 * many :]
        here = lax.axis_index(axis)

        def rows(k, who):
            return pl.ds(pl.multiple_of(who * chunks[k], chunks[k]), chunks[k])

        greet_all(axis, count, here)
        copies = {}
        for d in range(1, count):
            peer = lax.rem(here + d, count)
            for k in range(many):
                copies[k, d] = pltpu.make_async_remote_copy(
                    src_ref=ins[k].at[rows(k, peer)],
                    dst_ref=first[k].at[d - 1],
                    send_sem=send1.at[k, d - 1],
                    recv_sem=recv1.at[k, d - 1],
                    device_id={axis: peer},
                    device_id_type=MESH,
                )
                copies[k, d].start()
        for k in range(many):
            total = ins[k][rows(k, here)].astype(F32)
            for d in range(1, count):
                copies[k, d].wait()
                total = total + first[k][d - 1].astype(F32)
            mine[k][...] = total.astype(mine[k].dtype)
            for d in range(1, count):
                copies[k, d] = pltpu.make_async_remote_copy(
                    src_ref=mine[k],
                    dst_ref=second[k].at[d - 1],
                    send_sem=send2.at[k, d - 1],
                    recv_sem=recv2.at[k, d - 1],
                    device_id={axis: lax.rem(here + d, count)},
                    device_id_type=MESH,
                )
                copies[k, d].start()
            outs[k][rows(k, here)] = mine[k][...].astype(F32)
        for k in range(many):
            for d in range(1, count):
                copies[k, d].wait()
                outs[k][rows(k, lax.rem(here - d + count, count))] = second[k][d - 1].astype(F32)

    lanes = [a.shape[1] for a in arrays]
    slots = [
        pltpu.VMEM((count - 1, c, w), a.dtype) for a, c, w in zip(arrays, chunks, lanes)
    ]
    return pl.pallas_call(
        body,
        out_shape=tuple(jax.ShapeDtypeStruct(a.shape, F32) for a in arrays),
        in_specs=[pl.BlockSpec(memory_space=pltpu.VMEM)] * many,
        out_specs=tuple([pl.BlockSpec(memory_space=pltpu.VMEM)] * many),
        scratch_shapes=slots
        + slots
        + [pltpu.VMEM((c, w), a.dtype) for a, c, w in zip(arrays, chunks, lanes)]
        + [pltpu.SemaphoreType.DMA((many, count - 1))] * 4,
        compiler_params=pltpu.CompilerParams(
            collective_id=collective_id, has_side_effects=True, vmem_limit_bytes=VMEM_LIMIT
        ),
    )(*arrays)


PIECE = 16


def chain(states, decays, axis, collective_id):
    count = lax.axis_size(axis)
    kinds, depth, width = states.shape
    pieces = depth // PIECE
    routes = (((0, 0), (3, 1)), ((1, 1), (2, 0)))

    def body(own, decay, out, inbox, outbox, send, recv):
        here = lax.axis_index(axis)
        following = lax.rem(here + 1, count)
        previous = lax.rem(here - 1 + count, count)
        barrier = pltpu.get_barrier_semaphore()
        for who in (previous, following):
            pl.semaphore_signal(barrier, inc=1, device_id={axis: who}, device_id_type=MESH)
        pl.semaphore_wait(barrier, 2)

        def copy_of(way, j):
            return pltpu.make_async_remote_copy(
                src_ref=outbox.at[way, j],
                dst_ref=inbox.at[way, j],
                send_sem=send.at[way, j],
                recv_sem=recv.at[way, j],
                device_id={axis: following if way == 0 else previous},
                device_id_type=MESH,
            )

        def has_next(way):
            return here < count - 1 if way == 0 else here > 0

        def tick(t, carry):
            for way in range(2):
                rank = here if way == 0 else count - 1 - here
                j = t - rank

                @pl.when((j >= 0) & (j < pieces))
                def _(way=way, rank=rank, j=j):
                    @pl.when(rank > 0)
                    def _():
                        copy_of(way, j).wait_recv()

                    @pl.when(rank == 0)
                    def _():
                        inbox[way, j] = jnp.zeros((2, PIECE, width), BF)

                    for item, (kind, branch) in enumerate(routes[way]):
                        entering = inbox[way, j, item]
                        out[kind, j] = entering
                        outbox[way, j, item] = (
                            decay[branch : branch + 1, :] * entering.astype(F32)
                            + own[kind, j].astype(F32)
                        ).astype(BF)

                    @pl.when(has_next(way))
                    def _():
                        copy_of(way, j).start()

            return carry

        lax.fori_loop(0, count + pieces - 1, tick, 0)

        def finish(j, carry):
            for way in range(2):

                @pl.when(has_next(way))
                def _(way=way):
                    copy_of(way, j).wait_send()

            return carry

        lax.fori_loop(0, pieces, finish, 0)

    shape = (kinds, pieces, PIECE, width)
    box = pltpu.VMEM((2, pieces, 2, PIECE, width), BF)
    result = pl.pallas_call(
        body,
        out_shape=jax.ShapeDtypeStruct(shape, BF),
        in_specs=[pl.BlockSpec(memory_space=pltpu.VMEM)] * 2,
        out_specs=pl.BlockSpec(memory_space=pltpu.VMEM),
        scratch_shapes=[
            box,
            box,
            pltpu.SemaphoreType.DMA((2, pieces)),
            pltpu.SemaphoreType.DMA((2, pieces)),
        ],
        compiler_params=pltpu.CompilerParams(
            collective_id=collective_id, has_side_effects=True, vmem_limit_bytes=VMEM_LIMIT
        ),
    )(states.reshape(shape), decays)
    return result.reshape(states.shape)


def as_rows(values, unit):
    flat = jnp.concatenate([v.reshape(-1) for v in values])
    size = flat.shape[0]
    padded = -(-size // (128 * unit)) * (128 * unit)
    return jnp.pad(flat, (0, padded - size)).reshape(-1, 128)


def neighbours(value, axis, steps):
    count = lax.axis_size(axis)
    first, last = (max(0, -steps), min(count, count - steps))
    return lax.ppermute(value, axis, [(source, source + steps) for source in range(first, last)])


def round_keep(value):
    rounded = lax.optimization_barrier(value.astype(BF))
    return rounded.astype(F32)


def conv_pair(padded, conv_weight, conv_bias):
    radius = conv_weight.shape[0] - 1
    length = padded.shape[0] - 2 * radius
    forward = conv_bias
    backward = conv_bias
    for k in range(radius + 1):
        forward = forward + conv_weight[k] * padded[radius - k : radius - k + length]
        backward = backward + conv_weight[k] * padded[radius + k : radius + k + length]
    return forward, backward


def local(token_ids, table, norm_gain, conv_weight, conv_bias, weight_b, weight_c, step_weight,
          step_bias, log_rate, skip_gain, out_grad):
    rows = token_ids.shape[0]
    width = table.shape[1]
    vocab = table.shape[0]
    heads = step_bias.shape[0]
    state = weight_b.shape[1]
    features = width * lax.axis_size("fsdp")
    all_heads = step_weight.shape[1]
    radius = conv_weight.shape[0] - 1
    here = lax.axis_index("ctx")

    table_sums = lax.psum(jnp.sum(table * table, axis=1), "fsdp")
    marked = token_ids + 1
    before = neighbours(marked[rows - radius :], "ctx", 1)
    after = neighbours(marked[:radius], "ctx", -1)
    marks = jnp.concatenate([before, marked, after])
    inverse = lax.rsqrt(table_sums / features + 1e-05)[:, None]
    unit_table = table * inverse
    normed_table = (unit_table * norm_gain).astype(BF)
    onehot_pad = (marks[:, None] == jnp.arange(1, vocab + 1)[None, :]).astype(BF)
    padded = dot(onehot_pad, normed_table)
    pre_f, pre_r = conv_pair(padded, conv_weight, conv_bias)
    xf = jax.nn.silu(pre_f).astype(BF)
    xr = jax.nn.silu(pre_r).astype(BF)
    joined_w = jnp.concatenate([weight_b, weight_c, step_weight], axis=1)
    both_x = jnp.concatenate([xf, xr], axis=0)
    parts = dot(both_x, joined_w[:, : 2 * state]).astype(BF)
    raw_parts = dot(step_weight, both_x, 0, 1)
    half, raw_sums = exchange((parts, raw_parts), ("sum", "sum"), "fsdp", 1)
    first_head = lax.axis_index("fsdp") * heads
    raws = lax.dynamic_slice_in_dim(raw_sums, first_head, heads, 0).T
    bf, cf = half[:rows, :state], half[:rows, state:]
    br, cr = half[rows:, :state], half[rows:, state:]
    raw_f, raw_r = raws[:rows], raws[rows:]
    bias = step_bias[None]
    rate = log_rate[None]
    small = ((rows, heads), F32)
    one = ((1, heads), F32)
    ends = ((8, width), F32)
    states, cum_f, step_f, end_f, cum_r, step_r, end_r = whole_kernel(
        states_stage,
        [((4, state, width), BF), small, small, ends, small, small, ends],
        (raw_f, raw_r, bias, rate, xf, xr, bf, cf, br, cr, out_grad),
    )
    decays = jnp.concatenate([end_f[:1], end_r[:1]])
    chained = chain(states, decays, "ctx", 2)
    pairs = heads // 2

    def paired(value):
        return jnp.transpose(value.reshape(rows, pairs, 2), (1, 0, 2))

    cols = jnp.concatenate([paired(v) for v in (cum_f, cum_r, step_f, step_r)], axis=2)
    cut = jnp.transpose(cols[:, :, :4], (0, 2, 1))
    yf, yr, pf, pr, df, dr = intra_stage(cols, cut, xf, xr, out_grad, bf, cf, br, cr)
    mixer_out, d_fx, d_rx, d_bc, d_raw, d_bias, d_rate, d_skip = whole_kernel(
        joined_stage,
        [
            ((rows, width), BF),
            ((rows, width), F32),
            ((rows, width), F32),
            ((4, rows, state), BF),
            ((2, rows, heads), BF),
            one,
            one,
            one,
        ],
        (chained, yf, yr, pf, pr, df, dr, xf, xr, out_grad, bf, cf, br, cr, raw_f, raw_r,
         cum_f, cum_r, bias, rate, skip_gain[None]),
    )
    raw_rows = jnp.transpose(d_raw, (0, 2, 1)).reshape(2 * heads, rows)
    raw_rows = jnp.pad(raw_rows, ((0, -2 * heads % PIECE), (0, 0)))
    summed_bc, every = exchange((d_bc, raw_rows), ("sum", "gather"), "fsdp", 3)
    every_raw = [
        every[:, k * heads : (k + 1) * heads].reshape(all_heads, rows).T for k in range(2)
    ]
    back = jnp.concatenate(
        [
            jnp.concatenate([summed_bc[0], summed_bc[1], every_raw[0]], axis=1),
            jnp.concatenate([summed_bc[2], summed_bc[3], every_raw[1]], axis=1),
        ],
        axis=0,
    )
    into = dot(back, joined_w, 1, 1)
    grad_w = dot(both_x, back, 0, 0).astype(BF)

    def silu_back(pre, d_x):
        gate = jax.nn.sigmoid(pre)
        return d_x.astype(BF).astype(F32) * (gate * (1.0 + pre * (1.0 - gate)))

    pre_f, pre_r = conv_pair(padded, conv_weight, conv_bias)
    dp_f = silu_back(pre_f, d_fx + into[:rows])
    dp_r = silu_back(pre_r, d_rx + into[rows:])
    d_cb = jnp.sum(dp_f + dp_r, axis=0)
    d_cw = jnp.stack(
        [
            jnp.sum(
                dp_f * padded[radius - k : radius - k + rows]
                + dp_r * padded[radius + k : radius + k + rows],
                axis=0,
            )
            for k in range(radius + 1)
        ]
    )
    dp_f_after = neighbours(dp_f[:radius], "ctx", -1)
    dp_r_before = neighbours(dp_r[rows - radius :], "ctx", 1)
    long_f = jnp.concatenate([dp_f, dp_f_after], axis=0)
    long_r = jnp.concatenate([dp_r_before, dp_r], axis=0)
    center = 0.0
    for k in range(radius + 1):
        center = center + conv_weight[k] * (
            long_f[k : k + rows] + long_r[radius - k : radius - k + rows]
        )
    grad_normed = round_keep(center)
    onehot = (token_ids[:, None] == jnp.arange(vocab)[None, :]).astype(F32)
    scale = jnp.sum(onehot * inverse[:, 0], axis=1, keepdims=True)
    embedded = jnp.dot(onehot, table, precision=HI)
    grad_unit = grad_normed * norm_gain
    cross = lax.psum(jnp.sum(grad_unit * embedded, axis=1), "fsdp")[:, None]
    d_embedded = scale * grad_unit - embedded * (scale * scale * scale) * (cross / features)
    grad_embedded = d_embedded.astype(BF)
    d_table = jnp.dot(onehot.T, d_embedded, precision=HI)
    d_gain = jnp.sum(grad_normed * (embedded * scale), axis=0)
    parts = (d_table, d_gain, d_cw, d_cb, d_bias, d_rate, d_skip)
    shards = lax.axis_size("ctx")
    weight_rows, rest_rows = reduce_all(
        (as_rows((grad_w,), 16 * shards), as_rows(parts, 8 * shards)), "ctx", 4
    )
    grad_w = weight_rows.reshape(-1)[: grad_w.size].reshape(grad_w.shape)
    rest = rest_rows.reshape(-1)
    outs = []
    for part, shape in zip(
        parts,
        (d_table.shape, (width,), conv_weight.shape, (width,), (heads,), (heads,), (heads,)),
    ):
        outs.append(rest[: part.size].reshape(shape))
        rest = rest[part.size :]
    return (
        mixer_out,
        grad_embedded,
        *outs[:4],
        grad_w[:, :state],
        grad_w[:, state : 2 * state],
        grad_w[:, 2 * state :],
        *outs[4:],
    )


def solution(mesh):
    return jax.shard_map(
        local,
        mesh=mesh,
        in_specs=(
            P("ctx"),
            P(None, "fsdp"),
            P("fsdp"),
            P(None, "fsdp"),
            P("fsdp"),
            P("fsdp", None),
            P("fsdp", None),
            P("fsdp", None),
            P("fsdp"),
            P("fsdp"),
            P("fsdp"),
            P("ctx", "fsdp"),
        ),
        out_specs=(
            P("ctx", "fsdp"),
            P("ctx", "fsdp"),
            P(None, "fsdp"),
            P("fsdp"),
            P(None, "fsdp"),
            P("fsdp"),
            P("fsdp", None),
            P("fsdp", None),
            P("fsdp", None),
            P("fsdp"),
            P("fsdp"),
            P("fsdp"),
        ),
        check_vma=False,
    )
```

```python
import functools

import jax
import jax.numpy as jnp
from jax import lax
from jax.experimental import pallas as pl
from jax.experimental.pallas import tpu as pltpu
from jax.sharding import PartitionSpec as P

F32 = jnp.float32
BF = jnp.bfloat16
HI = lax.Precision.HIGHEST
VMEM_LIMIT = 56 * 1024 * 1024


def dot(a, b, ca=1, cb=0, precision=None):
    return lax.dot_general(
        a, b, (((ca,), (cb,)), ((), ())), precision=precision, preferred_element_type=F32
    )


def split_dot(value, sel, cb=0):
    hi = value.astype(BF)
    lo = (value - hi.astype(F32)).astype(BF)
    return dot(hi, sel, 1, cb) + dot(lo, sel, 1, cb)


def softplus(v):
    return jnp.maximum(v, 0.0) + jnp.log1p(jnp.exp(-jnp.abs(v)))


def selector(heads, width):
    per = width // heads
    row = lax.broadcasted_iota(jnp.int32, (heads, width), 0)
    col = lax.broadcasted_iota(jnp.int32, (heads, width), 1)
    return jnp.where((col >= row * per) & (col < row * per + per), 1.0, 0.0).astype(BF)


def order_mask(rows, reverse):
    t = lax.broadcasted_iota(jnp.int32, (rows, rows), 0)
    s = lax.broadcasted_iota(jnp.int32, (rows, rows), 1)
    return (s >= t) if reverse else (s <= t)


def whole_kernel(fn, outs, args):
    count = len(args)

    def body(*refs):
        results = fn(*[r[...] for r in refs[:count]])
        for ref, value in zip(refs[count:], results):
            ref[...] = value.astype(ref.dtype)

    return pl.pallas_call(
        body,
        out_shape=tuple(jax.ShapeDtypeStruct(s, d) for s, d in outs),
        compiler_params=pltpu.CompilerParams(vmem_limit_bytes=VMEM_LIMIT),
    )(*args)


def states_stage(raw_f, raw_r, bias, log_rate, xf, xr, bf, cf, br, cr, dy):
    rows, heads = raw_f.shape
    sel = selector(heads, xf.shape[1])
    rate = jnp.exp(log_rate)
    cols = []
    states = []
    dstates = []
    for raw, x, b, c, reverse in ((raw_f, xf, bf, cf, False), (raw_r, xr, br, cr, True)):
        step = softplus(raw + bias)
        logdec = -step * rate
        tri = jnp.where(order_mask(rows, reverse), 1.0, 0.0)
        cumul = dot(tri, logdec, precision=HI)
        end = jnp.sum(logdec, axis=0, keepdims=True)
        wt = jnp.exp(end - cumul) * step
        xs = (split_dot(wt, sel) * x.astype(F32)).astype(BF)
        states.append(dot(b, xs, 0, 0))
        gy = (split_dot(jnp.exp(cumul), sel) * dy.astype(F32)).astype(BF)
        dstates.append(dot(c, gy, 0, 0))
        wide_end = split_dot(jnp.broadcast_to(jnp.exp(end), (8, heads)), sel)
        cols += [cumul, step, wide_end]
    return (jnp.stack(states + dstates),) + tuple(cols)


def intra_kernel(cols_ref, cut_ref, xf_ref, xr_ref, dy_ref, bf_ref, cf_ref, br_ref, cr_ref,
                 yf_ref, yr_ref, pf_ref, pr_ref, df_ref, dr_ref, inner_f, inner_r):
    rows = xf_ref.shape[0]
    per = xf_ref.shape[1] // 2

    @pl.when(pl.program_id(0) == 0)
    def _():
        inner_f[...] = dot(cf_ref[...], bf_ref[...], 1, 1)
        inner_r[...] = dot(cr_ref[...], br_ref[...], 1, 1)
        df_ref[...] = jnp.zeros_like(df_ref)
        dr_ref[...] = jnp.zeros_like(dr_ref)

    dy = dy_ref[...]
    lane = lax.broadcasted_iota(jnp.int32, dy.shape, 1)
    zero = jnp.zeros_like(dy)
    cols = cols_ref[0]
    cut = cut_ref[0]
    for branch, (x_ref, inner, y_ref, p_ref, d_ref) in enumerate(
        ((xf_ref, inner_f, yf_ref, pf_ref, df_ref), (xr_ref, inner_r, yr_ref, pr_ref, dr_ref))
    ):
        mask = order_mask(rows, branch == 1)
        st = jnp.where(
            lane < per,
            cols[:, 4 + 2 * branch : 5 + 2 * branch],
            cols[:, 5 + 2 * branch : 6 + 2 * branch],
        )
        xs = (st * x_ref[...].astype(F32)).astype(BF)
        y = None
        p = None
        total = d_ref[...]
        for k in range(2):
            mine = (lane < per) if k == 0 else (lane >= per)
            at = 2 * branch + k
            spread = cols[:, at : at + 1] - cut[at : at + 1, :]
            decay = jnp.exp(jnp.where(mask, spread, -1e30))
            mixing = (inner[...] * decay).astype(BF)
            xs_k = jnp.where(mine, xs, zero)
            dy_k = jnp.where(mine, dy, zero)
            y_k = dot(mixing, xs_k)
            p_k = dot(mixing, dy_k, 0, 0)
            total = total + dot(dy, xs_k, 1, 1) * decay
            y = y_k if y is None else y + y_k
            p = p_k if p is None else p + p_k
        y_ref[...] = y
        p_ref[...] = p
        d_ref[...] = total


def intra_stage(cols, cut, xf, xr, dy, bf, cf, br, cr):
    rows, width = xf.shape
    pairs = cols.shape[0]
    lanes = width // pairs
    wide = pl.BlockSpec((rows, lanes), lambda j: (0, j))
    small = pl.BlockSpec(bf.shape, lambda j: (0, 0))
    square = pl.BlockSpec((rows, rows), lambda j: (0, 0))
    return pl.pallas_call(
        intra_kernel,
        grid=(pairs,),
        in_specs=[
            pl.BlockSpec((1, rows, 8), lambda j: (j, 0, 0)),
            pl.BlockSpec((1, 4, rows), lambda j: (j, 0, 0)),
            wide,
            wide,
            wide,
            small,
            small,
            small,
            small,
        ],
        out_specs=[wide, wide, wide, wide, square, square],
        out_shape=[jax.ShapeDtypeStruct((rows, width), F32)] * 4
        + [jax.ShapeDtypeStruct((rows, rows), F32)] * 2,
        scratch_shapes=[pltpu.VMEM((rows, rows), F32), pltpu.VMEM((rows, rows), F32)],
        compiler_params=pltpu.CompilerParams(vmem_limit_bytes=VMEM_LIMIT),
    )(cols, cut, xf, xr, dy, bf, cf, br, cr)


def joined_stage(chained, yf, yr, pf, pr, df, dr, xf, xr, dy_half, bf, cf, br, cr,
                 raw_f, raw_r, cum_f, cum_r, bias, log_rate, skip):
    rows, heads = raw_f.shape
    sel = selector(heads, xf.shape[1])
    rate = jnp.exp(log_rate)
    dy = dy_half.astype(F32)
    channel = split_dot(jnp.broadcast_to(skip, (8, heads)), sel)[:1]
    both = xf.astype(F32) + xr.astype(F32)
    mixed = channel * both
    direct = channel * dy
    d_skip = jnp.sum(split_dot(dy * both, sel, 1), axis=0, keepdims=True)
    results = []
    d_bias = 0.0
    d_rate = 0.0
    for k, (intra, p, square, x_half, b, c, raw, cumul) in enumerate(
        ((yf, pf, df, xf, bf, cf, raw_f, cum_f), (yr, pr, dr, xr, br, cr, raw_r, cum_r))
    ):
        reverse = k == 1
        start = chained[k]
        leaving = chained[2 + k]
        x = x_half.astype(F32)
        shifted = raw + bias
        step = softplus(shifted)
        logdec = -step * rate
        end = jnp.sum(logdec, axis=0, keepdims=True)
        grow = split_dot(jnp.exp(cumul), sel)
        fade = split_dot(jnp.exp(end - cumul), sel)
        wide_step = split_dot(step, sel)
        start_half = start.astype(BF)
        leaving_half = leaving.astype(BF)
        y = intra + grow * dot(c, start_half)
        mixed = mixed + y
        state_back = fade * dot(b, leaving_half)
        q = p + state_back
        x_step = wide_step * x
        d_x = wide_step * q + direct
        square_half = square.astype(BF)
        gy = (grow * dy).astype(BF)
        d_c = dot(square_half, b) + dot(gy, start_half, 1, 1)
        xs2 = (x_step * fade).astype(BF)
        d_b = dot(square_half, c, 0, 0) + dot(xs2, leaving_half, 1, 1)
        d_step = split_dot(x * q, sel, 1)
        through = split_dot(x_step * state_back, sel, 1)
        own = x_step.astype(BF).astype(F32) * p
        d_cumul = split_dot(dy * y - own, sel, 1) - through
        pair = split_dot(leaving * start, sel, 1)
        d_end = jnp.sum(through, axis=0, keepdims=True) + jnp.exp(end) * jnp.sum(
            pair, axis=0, keepdims=True
        )
        tri = jnp.where(order_mask(rows, reverse), 1.0, 0.0)
        d_log = dot(tri, d_cumul, 0, 0, precision=HI) + d_end
        d_step = d_step - rate * d_log
        d_raw = d_step / (1.0 + jnp.exp(-shifted))
        d_bias = d_bias + jnp.sum(d_raw, axis=0, keepdims=True)
        d_rate = d_rate + jnp.sum(d_log * logdec, axis=0, keepdims=True)
        results.append((d_x, d_b, d_c, d_raw))
    (fx, fb, fc, fs), (rx, rb, rc, rs) = results
    return mixed, fx, rx, jnp.stack([fb, fc, rb, rc]), jnp.stack([fs, rs]), d_bias, d_rate, d_skip


MESH = pl.DeviceIdType.MESH


def greet_all(axis, count, here):
    barrier = pltpu.get_barrier_semaphore()
    for d in range(1, count):
        pl.semaphore_signal(
            barrier, inc=1, device_id={axis: lax.rem(here + d, count)}, device_id_type=MESH
        )
    pl.semaphore_wait(barrier, count - 1)


def exchange(arrays, modes, axis, collective_id):
    count = lax.axis_size(axis)
    many = len(arrays)

    def body(*refs):
        ins, outs, bufs = refs[:many], refs[many : 2 * many], refs[2 * many : 3 * many]
        send, recv = refs[3 * many :]
        here = lax.axis_index(axis)
        greet_all(axis, count, here)
        copies = []
        for d in range(1, count):
            for k in range(many):
                copy = pltpu.make_async_remote_copy(
                    src_ref=ins[k].at[lax.rem(here + d, count)] if modes[k] == "scatter" else ins[k],
                    dst_ref=bufs[k].at[d - 1],
                    send_sem=send.at[k, d - 1],
                    recv_sem=recv.at[k, d - 1],
                    device_id={axis: lax.rem(here + d, count)},
                    device_id_type=MESH,
                )
                copy.start()
                copies.append(copy)
        for copy in copies:
            copy.wait()
        for k in range(many):
            if modes[k] != "gather":
                own = ins[k][here] if modes[k] == "scatter" else ins[k][...]
                total = own.astype(F32)
                for d in range(1, count):
                    total = total + bufs[k][d - 1].astype(F32)
                outs[k][...] = total.astype(outs[k].dtype)
            else:
                outs[k][here] = ins[k][...]
                for d in range(1, count):
                    outs[k][lax.rem(here - d + count, count)] = bufs[k][d - 1]

    blocks = [a.shape[1:] if m == "scatter" else a.shape for a, m in zip(arrays, modes)]
    shapes = [
        jax.ShapeDtypeStruct((count,) + a.shape if m == "gather" else blocks[i], a.dtype)
        for i, (a, m) in enumerate(zip(arrays, modes))
    ]
    return pl.pallas_call(
        body,
        out_shape=tuple(shapes),
        in_specs=[pl.BlockSpec(memory_space=pltpu.VMEM)] * many,
        out_specs=tuple([pl.BlockSpec(memory_space=pltpu.VMEM)] * many),
        scratch_shapes=[pltpu.VMEM((count - 1,) + b, a.dtype) for a, b in zip(arrays, blocks)]
        + [pltpu.SemaphoreType.DMA((many, count - 1)), pltpu.SemaphoreType.DMA((many, count - 1))],
        compiler_params=pltpu.CompilerParams(
            collective_id=collective_id, has_side_effects=True, vmem_limit_bytes=VMEM_LIMIT
        ),
    )(*arrays)


def reduce_all(arrays, axis, collective_id):
    count = lax.axis_size(axis)
    many = len(arrays)
    chunks = [a.shape[0] // count for a in arrays]

    def body(*refs):
        ins, outs = refs[:many], refs[many : 2 * many]
        first, second = refs[2 * many : 3 * many], refs[3 * many : 4 * many]
        mine = refs[4 * many : 5 * many]
        send1, recv1, send2, recv2 = refs[5 * many :]
        here = lax.axis_index(axis)

        def rows(k, who):
            return pl.ds(pl.multiple_of(who * chunks[k], chunks[k]), chunks[k])

        greet_all(axis, count, here)
        copies = {}
        for d in range(1, count):
            peer = lax.rem(here + d, count)
            for k in range(many):
                copies[k, d] = pltpu.make_async_remote_copy(
                    src_ref=ins[k].at[rows(k, peer)],
                    dst_ref=first[k].at[d - 1],
                    send_sem=send1.at[k, d - 1],
                    recv_sem=recv1.at[k, d - 1],
                    device_id={axis: peer},
                    device_id_type=MESH,
                )
                copies[k, d].start()
        for k in range(many):
            total = ins[k][rows(k, here)].astype(F32)
            for d in range(1, count):
                copies[k, d].wait()
                total = total + first[k][d - 1].astype(F32)
            mine[k][...] = total.astype(mine[k].dtype)
            for d in range(1, count):
                copies[k, d] = pltpu.make_async_remote_copy(
                    src_ref=mine[k],
                    dst_ref=second[k].at[d - 1],
                    send_sem=send2.at[k, d - 1],
                    recv_sem=recv2.at[k, d - 1],
                    device_id={axis: lax.rem(here + d, count)},
                    device_id_type=MESH,
                )
                copies[k, d].start()
            outs[k][rows(k, here)] = mine[k][...].astype(F32)
        for k in range(many):
            for d in range(1, count):
                copies[k, d].wait()
                outs[k][rows(k, lax.rem(here - d + count, count))] = second[k][d - 1].astype(F32)

    lanes = [a.shape[1] for a in arrays]
    slots = [
        pltpu.VMEM((count - 1, c, w), a.dtype) for a, c, w in zip(arrays, chunks, lanes)
    ]
    return pl.pallas_call(
        body,
        out_shape=tuple(jax.ShapeDtypeStruct(a.shape, F32) for a in arrays),
        in_specs=[pl.BlockSpec(memory_space=pltpu.VMEM)] * many,
        out_specs=tuple([pl.BlockSpec(memory_space=pltpu.VMEM)] * many),
        scratch_shapes=slots
        + slots
        + [pltpu.VMEM((c, w), a.dtype) for a, c, w in zip(arrays, chunks, lanes)]
        + [pltpu.SemaphoreType.DMA((many, count - 1))] * 4,
        compiler_params=pltpu.CompilerParams(
            collective_id=collective_id, has_side_effects=True, vmem_limit_bytes=VMEM_LIMIT
        ),
    )(*arrays)


PIECE = 16


def chain(states, decays, axis, collective_id):
    count = lax.axis_size(axis)
    kinds, depth, width = states.shape
    pieces = depth // PIECE
    routes = (((0, 0), (3, 1)), ((1, 1), (2, 0)))

    def body(own, decay, out, inbox, outbox, send, recv):
        here = lax.axis_index(axis)
        following = lax.rem(here + 1, count)
        previous = lax.rem(here - 1 + count, count)
        barrier = pltpu.get_barrier_semaphore()
        for who in (previous, following):
            pl.semaphore_signal(barrier, inc=1, device_id={axis: who}, device_id_type=MESH)
        pl.semaphore_wait(barrier, 2)

        def copy_of(way, j):
            return pltpu.make_async_remote_copy(
                src_ref=outbox.at[way, j],
                dst_ref=inbox.at[way, j],
                send_sem=send.at[way, j],
                recv_sem=recv.at[way, j],
                device_id={axis: following if way == 0 else previous},
                device_id_type=MESH,
            )

        def has_next(way):
            return here < count - 1 if way == 0 else here > 0

        def tick(t, carry):
            for way in range(2):
                rank = here if way == 0 else count - 1 - here
                j = t - rank

                @pl.when((j >= 0) & (j < pieces))
                def _(way=way, rank=rank, j=j):
                    @pl.when(rank > 0)
                    def _():
                        copy_of(way, j).wait_recv()

                    @pl.when(rank == 0)
                    def _():
                        inbox[way, j] = jnp.zeros((2, PIECE, width), BF)

                    for item, (kind, branch) in enumerate(routes[way]):
                        entering = inbox[way, j, item]
                        out[kind, j] = entering
                        outbox[way, j, item] = (
                            decay[branch : branch + 1, :] * entering.astype(F32)
                            + own[kind, j].astype(F32)
                        ).astype(BF)

                    @pl.when(has_next(way))
                    def _():
                        copy_of(way, j).start()

            return carry

        lax.fori_loop(0, count + pieces - 1, tick, 0)

        def finish(j, carry):
            for way in range(2):

                @pl.when(has_next(way))
                def _(way=way):
                    copy_of(way, j).wait_send()

            return carry

        lax.fori_loop(0, pieces, finish, 0)

    shape = (kinds, pieces, PIECE, width)
    box = pltpu.VMEM((2, pieces, 2, PIECE, width), BF)
    result = pl.pallas_call(
        body,
        out_shape=jax.ShapeDtypeStruct(shape, BF),
        in_specs=[pl.BlockSpec(memory_space=pltpu.VMEM)] * 2,
        out_specs=pl.BlockSpec(memory_space=pltpu.VMEM),
        scratch_shapes=[
            box,
            box,
            pltpu.SemaphoreType.DMA((2, pieces)),
            pltpu.SemaphoreType.DMA((2, pieces)),
        ],
        compiler_params=pltpu.CompilerParams(
            collective_id=collective_id, has_side_effects=True, vmem_limit_bytes=VMEM_LIMIT
        ),
    )(states.reshape(shape), decays)
    return result.reshape(states.shape)


def as_rows(values, unit):
    flat = jnp.concatenate([v.reshape(-1) for v in values])
    size = flat.shape[0]
    padded = -(-size // (128 * unit)) * (128 * unit)
    return jnp.pad(flat, (0, padded - size)).reshape(-1, 128)


def neighbours(value, axis, steps):
    count = lax.axis_size(axis)
    first, last = (max(0, -steps), min(count, count - steps))
    return lax.ppermute(value, axis, [(source, source + steps) for source in range(first, last)])


def round_keep(value):
    rounded = lax.optimization_barrier(value.astype(BF))
    return rounded.astype(F32)


def conv_pair(padded, conv_weight, conv_bias):
    radius = conv_weight.shape[0] - 1
    length = padded.shape[0] - 2 * radius
    forward = conv_bias
    backward = conv_bias
    for k in range(radius + 1):
        forward = forward + conv_weight[k] * padded[radius - k : radius - k + length]
        backward = backward + conv_weight[k] * padded[radius + k : radius + k + length]
    return forward, backward


def local(token_ids, table, norm_gain, conv_weight, conv_bias, weight_b, weight_c, step_weight,
          step_bias, log_rate, skip_gain, out_grad):
    rows = token_ids.shape[0]
    width = table.shape[1]
    vocab = table.shape[0]
    heads = step_bias.shape[0]
    state = weight_b.shape[1]
    features = width * lax.axis_size("fsdp")
    all_heads = step_weight.shape[1]
    radius = conv_weight.shape[0] - 1
    here = lax.axis_index("ctx")

    table_sums = lax.psum(jnp.sum(table * table, axis=1), "fsdp")
    marked = token_ids + 1
    before = neighbours(marked[rows - radius :], "ctx", 1)
    after = neighbours(marked[:radius], "ctx", -1)
    marks = jnp.concatenate([before, marked, after])
    inverse = lax.rsqrt(table_sums / features + 1e-05)[:, None]
    unit_table = table * inverse
    normed_table = (unit_table * norm_gain).astype(BF)
    onehot_pad = (marks[:, None] == jnp.arange(1, vocab + 1)[None, :]).astype(BF)
    padded = dot(onehot_pad, normed_table)
    pre_f, pre_r = conv_pair(padded, conv_weight, conv_bias)
    xf = jax.nn.silu(pre_f).astype(BF)
    xr = jax.nn.silu(pre_r).astype(BF)
    joined_w = jnp.concatenate([weight_b, weight_c, step_weight], axis=1)
    both_x = jnp.concatenate([xf, xr], axis=0)
    parts = dot(both_x, joined_w[:, : 2 * state]).astype(BF)
    raw_parts = dot(step_weight, both_x, 0, 1)
    raw_parts = raw_parts.reshape(-1, heads, 2 * rows)
    half, raw_sums = exchange((parts, raw_parts), ("sum", "scatter"), "fsdp", 1)
    raws = raw_sums.T
    bf, cf = half[:rows, :state], half[:rows, state:]
    br, cr = half[rows:, :state], half[rows:, state:]
    raw_f, raw_r = raws[:rows], raws[rows:]
    bias = step_bias[None]
    rate = log_rate[None]
    small = ((rows, heads), F32)
    one = ((1, heads), F32)
    ends = ((8, width), F32)
    states, cum_f, step_f, end_f, cum_r, step_r, end_r = whole_kernel(
        states_stage,
        [((4, state, width), BF), small, small, ends, small, small, ends],
        (raw_f, raw_r, bias, rate, xf, xr, bf, cf, br, cr, out_grad),
    )
    decays = jnp.concatenate([end_f[:1], end_r[:1]])
    chained = chain(states, decays, "ctx", 2)
    pairs = heads // 2

    def paired(value):
        return jnp.transpose(value.reshape(rows, pairs, 2), (1, 0, 2))

    cols = jnp.concatenate([paired(v) for v in (cum_f, cum_r, step_f, step_r)], axis=2)
    cut = jnp.transpose(cols[:, :, :4], (0, 2, 1))
    yf, yr, pf, pr, df, dr = intra_stage(cols, cut, xf, xr, out_grad, bf, cf, br, cr)
    mixer_out, d_fx, d_rx, d_bc, d_raw, d_bias, d_rate, d_skip = whole_kernel(
        joined_stage,
        [
            ((rows, width), BF),
            ((rows, width), F32),
            ((rows, width), F32),
            ((4, rows, state), BF),
            ((2, rows, heads), BF),
            one,
            one,
            one,
        ],
        (chained, yf, yr, pf, pr, df, dr, xf, xr, out_grad, bf, cf, br, cr, raw_f, raw_r,
         cum_f, cum_r, bias, rate, skip_gain[None]),
    )
    raw_rows = jnp.transpose(d_raw, (0, 2, 1)).reshape(2 * heads, rows)
    raw_rows = jnp.pad(raw_rows, ((0, -2 * heads % PIECE), (0, 0)))
    summed_bc, every = exchange((d_bc, raw_rows), ("sum", "gather"), "fsdp", 3)
    every_raw = [
        every[:, k * heads : (k + 1) * heads].reshape(all_heads, rows).T for k in range(2)
    ]
    back = jnp.concatenate(
        [
            jnp.concatenate([summed_bc[0], summed_bc[1], every_raw[0]], axis=1),
            jnp.concatenate([summed_bc[2], summed_bc[3], every_raw[1]], axis=1),
        ],
        axis=0,
    )
    into = dot(back, joined_w, 1, 1)
    grad_w = dot(both_x, back, 0, 0).astype(BF)

    def silu_back(pre, d_x):
        gate = jax.nn.sigmoid(pre)
        return d_x.astype(BF).astype(F32) * (gate * (1.0 + pre * (1.0 - gate)))

    pre_f, pre_r = conv_pair(padded, conv_weight, conv_bias)
    dp_f = silu_back(pre_f, d_fx + into[:rows])
    dp_r = silu_back(pre_r, d_rx + into[rows:])
    d_cb = jnp.sum(dp_f + dp_r, axis=0)
    d_cw = jnp.stack(
        [
            jnp.sum(
                dp_f * padded[radius - k : radius - k + rows]
                + dp_r * padded[radius + k : radius + k + rows],
                axis=0,
            )
            for k in range(radius + 1)
        ]
    )
    dp_f_after = neighbours(dp_f[:radius], "ctx", -1)
    dp_r_before = neighbours(dp_r[rows - radius :], "ctx", 1)
    long_f = jnp.concatenate([dp_f, dp_f_after], axis=0)
    long_r = jnp.concatenate([dp_r_before, dp_r], axis=0)
    center = 0.0
    for k in range(radius + 1):
        center = center + conv_weight[k] * (
            long_f[k : k + rows] + long_r[radius - k : radius - k + rows]
        )
    grad_normed = round_keep(center)
    onehot = (token_ids[:, None] == jnp.arange(vocab)[None, :]).astype(F32)
    scale = jnp.sum(onehot * inverse[:, 0], axis=1, keepdims=True)
    embedded = jnp.dot(onehot, table, precision=HI)
    grad_unit = grad_normed * norm_gain
    cross = lax.psum(jnp.sum(grad_unit * embedded, axis=1), "fsdp")[:, None]
    d_embedded = scale * grad_unit - embedded * (scale * scale * scale) * (cross / features)
    grad_embedded = d_embedded.astype(BF)
    d_table = jnp.dot(onehot.T, d_embedded, precision=HI)
    d_gain = jnp.sum(grad_normed * (embedded * scale), axis=0)
    parts = (d_table, d_gain, d_cw, d_cb, d_bias, d_rate, d_skip)
    shards = lax.axis_size("ctx")
    weight_rows, rest_rows = reduce_all(
        (as_rows((grad_w,), 16 * shards), as_rows(parts, 8 * shards)), "ctx", 4
    )
    grad_w = weight_rows.reshape(-1)[: grad_w.size].reshape(grad_w.shape)
    rest = rest_rows.reshape(-1)
    outs = []
    for part, shape in zip(
        parts,
        (d_table.shape, (width,), conv_weight.shape, (width,), (heads,), (heads,), (heads,)),
    ):
        outs.append(rest[: part.size].reshape(shape))
        rest = rest[part.size :]
    return (
        mixer_out,
        grad_embedded,
        *outs[:4],
        grad_w[:, :state],
        grad_w[:, state : 2 * state],
        grad_w[:, 2 * state :],
        *outs[4:],
    )


def solution(mesh):
    return jax.shard_map(
        local,
        mesh=mesh,
        in_specs=(
            P("ctx"),
            P(None, "fsdp"),
            P("fsdp"),
            P(None, "fsdp"),
            P("fsdp"),
            P("fsdp", None),
            P("fsdp", None),
            P("fsdp", None),
            P("fsdp"),
            P("fsdp"),
            P("fsdp"),
            P("ctx", "fsdp"),
        ),
        out_specs=(
            P("ctx", "fsdp"),
            P("ctx", "fsdp"),
            P(None, "fsdp"),
            P("fsdp"),
            P(None, "fsdp"),
            P("fsdp"),
            P("fsdp", None),
            P("fsdp", None),
            P("fsdp", None),
            P("fsdp"),
            P("fsdp"),
            P("fsdp"),
        ),
        check_vma=False,
    )
```
